32 devices in a mesh: seq: 16 (over z, y, x), head: 2 (over core).
Axes of the slice: x: 2, y: 2, z: 4, core: 2. Of those that a mesh axis runs over, the one named last changes fastest.
Arguments:
- queries: bfloat16 [2304, 2048], P('seq', 'head'), may hold values from -24 to 24
- key_matrix: bfloat16 [2304, 256], P('seq', 'head'), may hold values from -4 to 4
- value_matrix: bfloat16 [2304, 256], P('seq', 'head'), may hold values from -6 to 6
- query_feature_weight: bfloat16 [128, 1024], P(None, 'head'), may hold values from -0.5 to 0.5
- key_feature_weight: bfloat16 [128, 128], P(None, 'head'), may hold values from -0.5 to 0.5
Outputs:
- student_out: bfloat16 [2304, 2048], P('seq', 'head')
- query_map_grad: float32 [128, 1024], P(None, 'head')
- key_weight_gradient: float32 [128, 128], P(None, 'head')
- transfer_loss: float32 [], replicated
The draws below stay inside these ranges and needn't reach their ends.
All inputs are finite; a program needn't handle non-finite values.
Results may differ from the reference program's by a relative error of at most 0.008.
Values may be sent and summed in bfloat16 or wider, within the bound.
No kernel may reach another device: no remote copies, remote signals or barrier semaphores. Data moves between devices by JAX's collectives and lax.ppermute only.
A program may use at most 128 MiB of HBM per device.

```python
import jax
import jax.numpy as jnp
from jax import lax

HEAD_SIZE = 128
GROUP_QUERIES = 8
HALF_FEATURES = 64
TOK_DEV = 144
KEY_VALUE_HEADS = 2
QUERY_HEADS = 16
SEGMENT_TOKENS = 2304


def query_key_pair(key):
    base_key = jax.random.fold_in(key, 7)
    key_portion, query_part = jax.random.split(base_key)
    key_numbers = jax.random.truncated_normal(key_portion, -4.0, 4.0, (SEGMENT_TOKENS, KEY_VALUE_HEADS * HEAD_SIZE), jnp.float32)
    query_vals = jax.random.truncated_normal(query_part, -4.0, 4.0, (SEGMENT_TOKENS, QUERY_HEADS * HEAD_SIZE), jnp.float32)
    return (query_vals, key_numbers)


def draw_queries(key, part):
    return query_key_pair(key)[0].astype(jnp.bfloat16)


def draw_key_matrix(key, part):
    return query_key_pair(key)[1].astype(jnp.bfloat16)


def level_of(own_key, extent, cuts, low, largest):
    def one(dim, shards_of):
        draws = jax.random.uniform(jax.random.fold_in(jax.random.fold_in(own_key, 6), dim), (shards_of,), jnp.float32, low / len(cuts), largest / len(cuts))
        return jnp.repeat(jnp.exp(draws), extent[dim] // shards_of).reshape((-1,) + (1,) * (len(extent) - dim - 1))

    gain = one(*cuts[0])
    for cut in cuts[1:]:
        gain = gain * one(*cut)
    return gain


def noise(own_key, dims, width, reach, cuts=(), kind=jnp.bfloat16):
    result = jax.random.normal(own_key, dims, jnp.float32) * width
    if len(cuts) > 0:
        result = level_of(own_key, dims, cuts, -0.22, 0.18) * result
    return jnp.clip(result, min=-reach, max=reach).astype(kind)


def setup_inputs(seed: int = 0) -> dict:
    key_list = jax.random.split(jax.random.key(seed), 6)
    queries = draw_queries(jax.random.fold_in(key_list[5], 71), 0)
    key_matrix = draw_key_matrix(jax.random.fold_in(key_list[5], 71), 0)
    value_matrix = noise(key_list[2], (SEGMENT_TOKENS, KEY_VALUE_HEADS * HEAD_SIZE), 1.0, 6.0, ((0, 16), (1, 2)))
    query_feature_weight = noise(key_list[3], (HEAD_SIZE, QUERY_HEADS * HALF_FEATURES), HEAD_SIZE ** -0.5, 0.5, ((1, 2),))
    key_feature_weight = noise(key_list[4], (HEAD_SIZE, KEY_VALUE_HEADS * HALF_FEATURES), HEAD_SIZE ** -0.5, 0.5, ((1, 2),))
    return {"queries": queries, "key_matrix": key_matrix, "value_matrix": value_matrix, "query_feature_weight": query_feature_weight, "key_feature_weight": key_feature_weight}


def rounded(array):
    return lax.optimization_barrier(array.astype(jnp.bfloat16)).astype(jnp.float32)


def feature_pair(logits):
    plus_half = jax.nn.softmax(logits, axis=-1)
    minus_half = jax.nn.softmax(-logits, axis=-1)
    return plus_half, minus_half


def pair_backward(plus_half, minus_half, d_features):
    feat_count = plus_half.shape[-1]
    d_plus = d_features[..., :feat_count]
    d_minus = d_features[..., feat_count:]
    inner_plus = jnp.sum(d_plus * plus_half, axis=-1, keepdims=True)
    inner_minus = jnp.sum(d_minus * minus_half, axis=-1, keepdims=True)
    return plus_half * (d_plus - inner_plus) - minus_half * (d_minus - inner_minus)


def exclusive(array):
    totals = jnp.cumsum(array, axis=0)
    return jnp.concatenate([jnp.zeros_like(array[:1]), totals[:-1]], axis=0)


def teacher_head(query_head, key_head, value_head):
    blocks = SEGMENT_TOKENS // TOK_DEV
    highest = lax.Precision.HIGHEST
    key_wide = key_head.astype(jnp.float32)
    value_wide = value_head.astype(jnp.float32)
    key_pos = jnp.arange(SEGMENT_TOKENS, dtype=jnp.int32)
    query_blocks = query_head.reshape(blocks, TOK_DEV, GROUP_QUERIES, HEAD_SIZE)

    def one_block(inputs):
        row_block, block_index = inputs
        scores = jnp.einsum("tgd,sd->gts", row_block.astype(jnp.float32), key_wide, precision=highest) * (HEAD_SIZE ** -0.5)
        query_pos = block_index * TOK_DEV + jnp.arange(TOK_DEV, dtype=jnp.int32)
        visible = key_pos[None, None, :] <= query_pos[None, :, None]
        masked = jnp.where(visible, scores, -jnp.inf)
        row_max = jnp.max(masked, axis=-1, keepdims=True)
        exponent = jnp.exp(masked - row_max)
        row_sum = jnp.sum(exponent, axis=-1)
        mixed_rows = jnp.einsum("gts,sd->gtd", rounded(exponent), value_wide, precision=highest) / row_sum[..., None]
        return mixed_rows.astype(jnp.bfloat16)

    return lax.map(one_block, (query_blocks, jnp.arange(blocks, dtype=jnp.int32)))


def student_head(query_head, key_head, value_head, query_map_head, key_map_head, teacher_blocks):
    blocks = SEGMENT_TOKENS // TOK_DEV
    highest = lax.Precision.HIGHEST
    query_wide = query_head.astype(jnp.float32)
    key_wide = key_head.astype(jnp.float32)
    value_wide = value_head.astype(jnp.float32).reshape(blocks, TOK_DEV, HEAD_SIZE)
    query_logits = jnp.einsum("sgd,dgf->gsf", query_wide, query_map_head.astype(jnp.float32), precision=highest)
    query_plus, query_minus = feature_pair(query_logits)
    query_phi = rounded(jnp.concatenate([query_plus, query_minus], axis=-1))
    phi_blocks = query_phi.reshape(GROUP_QUERIES, blocks, TOK_DEV, 2 * HALF_FEATURES).transpose(1, 0, 2, 3)
    key_logits = jnp.einsum("sd,df->sf", key_wide, key_map_head.astype(jnp.float32), precision=highest)
    key_plus, key_minus = feature_pair(key_logits)
    key_phi = rounded(jnp.concatenate([key_plus, key_minus], axis=-1)).reshape(blocks, TOK_DEV, 2 * HALF_FEATURES)
    block_state = jnp.einsum("ntf,ntd->nfd", key_phi, value_wide, precision=highest)
    block_norm = jnp.sum(key_phi, axis=1)
    prefix_state = exclusive(block_state)
    prefix_norm = exclusive(block_norm)
    prefix_low = rounded(prefix_state)
    token_index = jnp.arange(TOK_DEV, dtype=jnp.int32)
    causal = token_index[None, :] <= token_index[:, None]
    intra_scores = jnp.where(causal, jnp.einsum("ngtf,nsf->ngts", phi_blocks, key_phi, precision=highest), 0.0)
    numerator = jnp.einsum("ngts,nsd->ngtd", rounded(intra_scores), value_wide, precision=highest)
    numerator = numerator + jnp.einsum("ngtf,nfd->ngtd", phi_blocks, prefix_low, precision=highest)
    denominator = jnp.sum(intra_scores, axis=-1) + jnp.einsum("ngtf,nf->ngt", phi_blocks, prefix_norm, precision=highest)
    student = numerator / denominator[..., None]
    target = teacher_blocks.astype(jnp.float32)
    differ = student - target
    loss_part = jnp.sum(differ * differ)
    grad_out = 2.0 * differ / SEGMENT_TOKENS
    numer_grad = grad_out / denominator[..., None]
    denom_grad = -jnp.sum(grad_out * student, axis=-1) / denominator
    numer_low = rounded(numer_grad)
    coupling = jnp.einsum("ngtd,nsd->ngts", numer_low, value_wide, precision=highest) + denom_grad[..., None]
    coupling_low = rounded(jnp.where(causal, coupling, 0.0))
    later_state = jnp.einsum("ngtf,ngtd->nfd", phi_blocks, numer_low, precision=highest)
    later_norm = jnp.einsum("ngtf,ngt->nf", phi_blocks, denom_grad, precision=highest)
    suffix_low = rounded(exclusive(later_state[::-1])[::-1])
    suffix_norm = exclusive(later_norm[::-1])[::-1]
    query_dphi = jnp.einsum("ngts,nsf->ngtf", coupling_low, key_phi, precision=highest)
    query_dphi = query_dphi + jnp.einsum("ngtd,nfd->ngtf", numer_low, prefix_low, precision=highest)
    query_dphi = query_dphi + denom_grad[..., None] * prefix_norm[:, None, None, :]
    key_dphi = jnp.einsum("ngts,ngtf->nsf", coupling_low, phi_blocks, precision=highest)
    key_dphi = key_dphi + jnp.einsum("nsd,nfd->nsf", value_wide, suffix_low, precision=highest)
    key_dphi = key_dphi + suffix_norm[:, None, :]
    query_dphi_all = query_dphi.transpose(1, 0, 2, 3).reshape(GROUP_QUERIES, SEGMENT_TOKENS, 2 * HALF_FEATURES)
    query_dlogit = rounded(pair_backward(query_plus, query_minus, query_dphi_all))
    key_dlogit = rounded(pair_backward(key_plus, key_minus, key_dphi.reshape(SEGMENT_TOKENS, 2 * HALF_FEATURES)))
    query_grad = jnp.einsum("sgd,gsf->dgf", query_wide, query_dlogit, precision=highest)
    key_grad = jnp.einsum("sd,sf->df", key_wide, key_dlogit, precision=highest)
    student_low = student.astype(jnp.bfloat16).transpose(0, 2, 1, 3).reshape(SEGMENT_TOKENS, GROUP_QUERIES, HEAD_SIZE)
    return student_low, query_grad, key_grad, loss_part


def reference(queries, key_matrix, value_matrix, query_feature_weight, key_feature_weight):
    query_pieces = queries.reshape(SEGMENT_TOKENS, KEY_VALUE_HEADS, GROUP_QUERIES, HEAD_SIZE).transpose(1, 0, 2, 3)
    key_pieces = key_matrix.reshape(SEGMENT_TOKENS, KEY_VALUE_HEADS, HEAD_SIZE).transpose(1, 0, 2)
    value_pieces = value_matrix.reshape(SEGMENT_TOKENS, KEY_VALUE_HEADS, HEAD_SIZE).transpose(1, 0, 2)
    query_weight_pieces = query_feature_weight.reshape(HEAD_SIZE, KEY_VALUE_HEADS, GROUP_QUERIES, HALF_FEATURES).transpose(1, 0, 2, 3)
    key_weight_pieces = key_feature_weight.reshape(HEAD_SIZE, KEY_VALUE_HEADS, HALF_FEATURES).transpose(1, 0, 2)

    def per_head(inputs):
        query_head, key_head, value_head, query_map_head, key_map_head = inputs
        teacher_blocks = teacher_head(query_head, key_head, value_head)
        return student_head(query_head, key_head, value_head, query_map_head, key_map_head, teacher_blocks)

    student_all, query_grads, key_gradient_list, loss_parts = lax.map(per_head, (query_pieces, key_pieces, value_pieces, query_weight_pieces, key_weight_pieces))
    student_out = student_all.transpose(1, 0, 2, 3).reshape(SEGMENT_TOKENS, QUERY_HEADS * HEAD_SIZE)
    query_map_grad = query_grads.transpose(1, 0, 2, 3).reshape(HEAD_SIZE, QUERY_HEADS * HALF_FEATURES)
    key_weight_gradient = key_gradient_list.transpose(1, 0, 2).reshape(HEAD_SIZE, KEY_VALUE_HEADS * HALF_FEATURES)
    transfer_loss = jnp.sum(loss_parts) / SEGMENT_TOKENS
    return student_out, query_map_grad, key_weight_gradient, transfer_loss
```

```python
import functools

import jax
import jax.numpy as jnp
from jax import lax
from jax.experimental import pallas as pl
from jax.experimental.pallas import tpu as pltpu
from jax.sharding import PartitionSpec as P

HEAD_SIZE = 128
GROUP_QUERIES = 8
HALF_FEATURES = 64
LOG2_E = 1.4426950408889634
SCORE_SCALE = HEAD_SIZE ** (-0.5) * LOG2_E
NEG_LARGE = -1e30
FAR = 1e30
VMEM_BYTES = 56 * 1024 * 1024
LOW = jnp.bfloat16
WIDE = jnp.float32


def dot(a, b, a_dim=1, b_dim=0):
    return lax.dot_general(a, b, (((a_dim,), (b_dim,)), ((), ())), preferred_element_type=WIDE)


def softmax_pair(logits):
    high = jnp.max(logits, axis=0, keepdims=True)
    low = jnp.min(logits, axis=0, keepdims=True)
    plus = jnp.exp(logits - high)
    minus = jnp.exp(low - logits)
    return (
        plus * (1.0 / jnp.sum(plus, axis=0, keepdims=True)),
        minus * (1.0 / jnp.sum(minus, axis=0, keepdims=True)),
    )


def pair_backward(plus, minus, d_plus, d_minus):
    inner_plus = jnp.sum(d_plus * plus, axis=0, keepdims=True)
    inner_minus = jnp.sum(d_minus * minus, axis=0, keepdims=True)
    return plus * (d_plus - inner_plus) - minus * (d_minus - inner_minus)


def sizes(seq_count):
    inner = 4 if seq_count % 4 == 0 else (2 if seq_count % 2 == 0 else 1)
    return seq_count // inner, inner


def head_kernel(seq_total, outer, inner, tokens, tile, q_ref, wq_ref, wk_ref, *refs):
    kv_refs = refs[:inner]
    out_ref, sums_ref = refs[inner : inner + 2]
    (rows_ref, phi_ref, plus_ref, minus_ref, teach_ref, top_ref, total_ref) = refs[inner + 2 :]
    rows = GROUP_QUERIES * tokens
    place = lax.axis_index("seq")
    plane = place // inner
    spot = place % inner

    for h in range(GROUP_QUERIES):
        rows_ref[h * tokens : (h + 1) * tokens, :] = q_ref[:, h * HEAD_SIZE : (h + 1) * HEAD_SIZE]

    head_of = lax.broadcasted_iota(jnp.int32, (1, rows), 1) // tokens
    token_of = lax.broadcasted_iota(jnp.int32, (1, rows), 1) - head_of * tokens

    all_logits = dot(wq_ref[...].T, rows_ref[...], 1, 1)
    logits = all_logits[:HALF_FEATURES]
    for h in range(1, GROUP_QUERIES):
        logits = jnp.where(head_of == h, all_logits[h * HALF_FEATURES : (h + 1) * HALF_FEATURES], logits)
    plus, minus = softmax_pair(logits)
    plus_ref[...] = plus
    minus_ref[...] = minus
    phi_ref[:HALF_FEATURES] = plus.astype(LOW)
    phi_ref[HALF_FEATURES:] = minus.astype(LOW)

    key_axis = lax.broadcasted_iota(jnp.int32, (tokens, 1), 0)
    for m in range(inner):
        kv_ref = kv_refs[m]
        values_t = kv_ref[:, HEAD_SIZE:].T
        first_ok = True if m == 0 else (spot ^ m) < spot
        ok = [first_ok] + [plane >= d for d in range(1, outer)]

        for c in range(rows // tile):
            cols = slice(c * tile, (c + 1) * tile)
            queries = rows_ref[cols, :]
            scores, tops = [], []
            for d in range(outer):
                keys = kv_ref[d * tokens : (d + 1) * tokens, :HEAD_SIZE]
                one = dot(keys, queries, 1, 1) * SCORE_SCALE
                if m == 0 and d == 0:
                    one = jnp.where(key_axis <= token_of[:, cols], one, NEG_LARGE)
                top = jnp.max(one, axis=0, keepdims=True)
                if not (m == 0 and d == 0):
                    top = jnp.where(ok[d], top, NEG_LARGE)
                scores.append(one)
                tops.append(top)
            high = functools.reduce(jnp.maximum, tops)
            if m > 0:
                before = top_ref[:, cols]
                high = jnp.maximum(high, before)
                shrink = jnp.exp2(before - high)
            total = None
            weights = []
            for d in range(outer):
                shift = high if m == 0 and d == 0 else jnp.where(ok[d], high, FAR)
                weight = jnp.exp2(scores[d] - shift)
                part = jnp.sum(weight, axis=0, keepdims=True)
                total = part if total is None else total + part
                weights.append(weight.astype(LOW))
            mixed = dot(values_t, jnp.concatenate(weights, axis=0), 1, 0)
            if m > 0:
                total = total + total_ref[:, cols] * shrink
                mixed = mixed + teach_ref[:, cols] * shrink
            top_ref[:, cols] = high
            total_ref[:, cols] = total
            teach_ref[:, cols] = mixed

    wk_t = wk_ref[...].T
    key_parts = []
    prefix_state = jnp.zeros((2 * HALF_FEATURES, HEAD_SIZE), WIDE)
    prefix_norm = jnp.zeros((2 * HALF_FEATURES, 1), WIDE)
    key_count = outer * tokens
    lane = lax.broadcasted_iota(jnp.int32, (1, key_count), 1)
    for m in range(inner):
        keys = kv_refs[m][:, :HEAD_SIZE]
        k_plus, k_minus = softmax_pair(dot(wk_t, keys, 1, 1))
        k_phi = jnp.concatenate([k_plus, k_minus], axis=0)
        low_end = tokens if m == 0 else jnp.where((spot ^ m) < spot, 0, tokens)
        valid = (lane >= low_end) & (lane < (plane + 1) * tokens)
        kept = jnp.where(valid, k_phi, 0.0).astype(LOW)
        prefix_state = prefix_state + dot(kept, kv_refs[m][:, HEAD_SIZE:], 1, 0)
        prefix_norm = prefix_norm + jnp.sum(kept.astype(WIDE), axis=1, keepdims=True)
        if m == 0:
            own_phi = k_phi[:, :tokens].astype(LOW)
            own_pair = (k_plus[:, :tokens], k_minus[:, :tokens])
        key_parts.append((k_plus, k_minus, valid))
    prefix_low = prefix_state.astype(LOW)

    own_values = kv_refs[0][:tokens, HEAD_SIZE:]
    phi = phi_ref[...]
    causal = key_axis <= token_of
    own_phi_rows = own_phi.T
    intra = jnp.where(causal, dot(own_phi_rows, phi, 1, 0), 0.0)
    denominator = jnp.sum(intra, axis=0, keepdims=True) + jnp.sum(
        phi.astype(WIDE) * prefix_norm, axis=0, keepdims=True
    )
    numerator = dot(own_values.T, intra.astype(LOW), 1, 0) + dot(prefix_low.T, phi, 1, 0)
    inverse = 1.0 / denominator
    student = numerator * inverse
    teacher = (teach_ref[...] * (1.0 / total_ref[...])).astype(LOW)
    differ = student - teacher.astype(WIDE)
    loss = jnp.sum(differ * differ)
    turned = student.T.astype(LOW)
    for h in range(GROUP_QUERIES):
        out_ref[:, h * HEAD_SIZE : (h + 1) * HEAD_SIZE] = turned[h * tokens : (h + 1) * tokens]

    grad_scale = 2.0 / seq_total
    grad_out = differ * grad_scale
    numer_low = (grad_out * inverse).astype(LOW)
    denom_grad = -jnp.sum(grad_out * student, axis=0, keepdims=True) * inverse
    coupling = jnp.where(causal, dot(own_values, numer_low, 1, 0) + denom_grad, 0.0).astype(LOW)
    later_low = dot(phi, numer_low, 1, 1).astype(LOW)
    later_norm = jnp.sum(phi.astype(WIDE) * denom_grad, axis=1, keepdims=True)
    query_dphi = dot(own_phi, coupling, 1, 0) + dot(prefix_low, numer_low, 1, 0) + prefix_norm * denom_grad
    query_dlogit = pair_backward(
        plus_ref[...], minus_ref[...], query_dphi[:HALF_FEATURES], query_dphi[HALF_FEATURES:]
    ).astype(LOW)
    for h in range(GROUP_QUERIES):
        spread = jnp.where(head_of == h, query_dlogit, jnp.zeros((), LOW))
        sums_ref[h * HALF_FEATURES : (h + 1) * HALF_FEATURES, :] = dot(spread, rows_ref[...], 1, 0).astype(
            sums_ref.dtype
        )

    own_dphi = dot(phi, coupling, 1, 1)
    own_dlogit = pair_backward(*own_pair, own_dphi[:HALF_FEATURES], own_dphi[HALF_FEATURES:])
    key_grad = dot(own_dlogit.astype(LOW), kv_refs[0][:tokens, :HEAD_SIZE], 1, 0)
    for m in range(inner):
        k_plus, k_minus, valid = key_parts[m]
        dphi = dot(later_low, kv_refs[m][:, HEAD_SIZE:], 1, 1) + later_norm
        dlogit = pair_backward(k_plus, k_minus, dphi[:HALF_FEATURES], dphi[HALF_FEATURES:])
        dlogit = jnp.where(valid, dlogit, 0.0).astype(LOW)
        key_grad = key_grad + dot(dlogit, kv_refs[m][:, :HEAD_SIZE], 1, 0)
    base = GROUP_QUERIES * HALF_FEATURES
    sums_ref[base : base + HALF_FEATURES, :] = key_grad.astype(sums_ref.dtype)
    sums_ref[base + HALF_FEATURES :, :] = jnp.full(
        (sums_ref.shape[0] - base - HALF_FEATURES, HEAD_SIZE), loss, WIDE
    ).astype(sums_ref.dtype)


def run_head(queries, wq, wk, gathered, seq_total, outer, inner, tokens, sums_rows):
    rows = GROUP_QUERIES * tokens
    tile = next(w for w in (384, 256, 128, rows) if rows % w == 0)
    full = pl.BlockSpec(memory_space=pltpu.VMEM)
    return pl.pallas_call(
        functools.partial(head_kernel, seq_total, outer, inner, tokens, tile),
        out_shape=(
            jax.ShapeDtypeStruct((tokens, GROUP_QUERIES * HEAD_SIZE), LOW),
            jax.ShapeDtypeStruct((sums_rows, HEAD_SIZE), WIDE),
        ),
        in_specs=[full] * (3 + inner),
        out_specs=(full, full),
        scratch_shapes=[
            pltpu.VMEM((rows, HEAD_SIZE), LOW),
            pltpu.VMEM((2 * HALF_FEATURES, rows), LOW),
            pltpu.VMEM((HALF_FEATURES, rows), WIDE),
            pltpu.VMEM((HALF_FEATURES, rows), WIDE),
            pltpu.VMEM((HEAD_SIZE, rows), WIDE),
            pltpu.VMEM((1, rows), WIDE),
            pltpu.VMEM((1, rows), WIDE),
        ],
        compiler_params=pltpu.CompilerParams(vmem_limit_bytes=VMEM_BYTES),
    )(queries, wq, wk, *gathered)


def local(queries, key_matrix, value_matrix, query_feature_weight, key_feature_weight):
    tokens = queries.shape[0]
    local_heads = key_matrix.shape[1] // HEAD_SIZE
    seq_count = lax.axis_size("seq")
    head_count = lax.axis_size("head")
    outer, inner = sizes(seq_count)
    seq_total = tokens * seq_count

    def columns(array, head, width):
        return array if local_heads == 1 else array[:, head * width : (head + 1) * width]

    outs, sums = [], []
    for head in range(local_heads):
        own = jnp.concatenate(
            [columns(key_matrix, head, HEAD_SIZE), columns(value_matrix, head, HEAD_SIZE)], axis=1
        )
        column = [own] + [
            lax.ppermute(own, "seq", [(i, i + inner * d) for i in range(seq_count - inner * d)])
            for d in range(1, outer)
        ]
        column = jnp.concatenate(column, axis=0)
        gathered = [column] + [
            lax.ppermute(column, "seq", [(i, i ^ m) for i in range(seq_count)]) for m in range(1, inner)
        ]
        base = (GROUP_QUERIES + 1) * HALF_FEATURES
        sums_rows = -(-(base + 8) // (8 * inner)) * 8 * inner
        out, part = run_head(
            columns(queries, head, GROUP_QUERIES * HEAD_SIZE),
            columns(query_feature_weight, head, GROUP_QUERIES * HALF_FEATURES),
            columns(key_feature_weight, head, HALF_FEATURES),
            gathered,
            seq_total,
            outer,
            inner,
            tokens,
            sums_rows,
        )
        outs.append(out)
        sums.append(part)

    planes = [[z * inner + p for p in range(inner)] for z in range(outer)]
    lines = [[z * inner + p for z in range(outer)] for p in range(inner)]
    total = jnp.concatenate(sums, axis=0) if local_heads > 1 else sums[0]
    width = total.shape[0] // inner
    share = lax.all_to_all(total.reshape(inner, width, HEAD_SIZE), "seq", 0, 0, axis_index_groups=planes)
    share = jnp.sum(share, axis=0)
    share = lax.all_to_all(
        jnp.broadcast_to(share[None], (outer,) + share.shape), "seq", 0, 0, axis_index_groups=lines
    )
    share = jnp.sum(share, axis=0)
    total = lax.all_to_all(
        jnp.broadcast_to(share[None], (inner,) + share.shape), "seq", 0, 0, axis_index_groups=planes
    ).reshape(local_heads, -1, HEAD_SIZE)

    split = GROUP_QUERIES * HALF_FEATURES
    query_grad = jnp.concatenate([total[g, :split].T for g in range(local_heads)], axis=1)
    key_grad = jnp.concatenate([total[g, split : split + HALF_FEATURES].T for g in range(local_heads)], axis=1)
    loss = jnp.sum(total[:, split + HALF_FEATURES, 0])
    others = [
        lax.ppermute(loss, "head", [(i, (i + d) % head_count) for i in range(head_count)])
        for d in range(1, head_count)
    ]
    loss = functools.reduce(jnp.add, others, loss) / seq_total
    return (outs[0] if local_heads == 1 else jnp.concatenate(outs, axis=1), query_grad, key_grad, loss)


def solution(mesh):
    placed = (
        P("seq", "head"),
        P("seq", "head"),
        P("seq", "head"),
        P(None, "head"),
        P(None, "head"),
    )
    return jax.shard_map(
        local,
        mesh=mesh,
        in_specs=placed,
        out_specs=(P("seq", "head"), P(None, "head"), P(None, "head"), P()),
        check_vma=False,
    )
```
